32 devices in a mesh: slab: 8 (over z, y), grp: 4 (over x, core).
Axes of the slice: x: 2, y: 2, z: 4, core: 2. Of those that a mesh axis runs over, the one named last changes fastest.
Arguments:
- blocks: bfloat16 [4, 4, 128, 128, 128], P('grp', None, 'slab'), may hold values from -6 to 6
- coords: int32 [4, 8, 4, 2], P('grp', 'slab'), may hold values from 0 to 15
- counts: int32 [4, 8], P('grp', 'slab'), may hold values from 1 to 4, as said below
- omega1: bfloat16 [128, 512], replicated, may hold values from -0.5 to 0.5
- omega2: bfloat16 [2048, 512], replicated, may hold values from -0.5 to 0.5
- omega3: bfloat16 [2048, 512], replicated, may hold values from -0.125 to 0.125
Outputs:
- core_sketch: float32 [512, 512, 512], P(None, 'slab', 'grp')
The draws below stay inside these ranges and needn't reach their ends.
Inputs may be any that keep to these rules, and one draw needn't show every extreme that they name: counts[g, s] slots are live in the list of group g on slab s; slots from it on are ignored. Some list holds 4 live slots in every draw.
All inputs are finite; a program needn't handle non-finite values.
Results may differ from the reference program's by a relative error of at most 0.0041.
Values may be sent and summed in bfloat16 or wider, within the bound.
A program may use at most 128 MiB of HBM per device.

```python
import jax
import jax.numpy as jnp
from jax import lax

RANK = 512
BLK = 128
ROWS_DEV = 16
MAX_BLOCKS = 4
NBLK = 16
ROWS = 128
N_SLAB = 8
N_GRP = 4


def draw_counts(key, part):
    key_heavy = jax.random.fold_in(key, 11)
    key_big = jax.random.fold_in(key, 12)
    key_small = jax.random.fold_in(key, 13)
    key_top = jax.random.fold_in(key, 14)
    heavy = jax.random.randint(key_heavy, (N_SLAB,), 0, N_GRP)
    bigger = jax.random.randint(key_big, (N_SLAB,), MAX_BLOCKS // 2, MAX_BLOCKS + 1)
    smaller = jax.random.randint(key_small, (N_GRP, N_SLAB), 1, MAX_BLOCKS // 4 + 1)
    group_ids = jnp.arange(N_GRP)[:, None]
    slab_ids = jnp.arange(N_SLAB)[None, :]
    is_heavy = group_ids == heavy[None, :]
    counts = jnp.where(is_heavy, bigger[None, :], smaller)
    top_slab = jax.random.randint(key_top, (), 0, N_SLAB)
    counts = jnp.where(is_heavy & (slab_ids == top_slab), MAX_BLOCKS, counts)
    return counts.astype(jnp.int32)


def touch_ends(drawn, stream_key, least, top_value):
    longest = drawn.shape.index(max(drawn.shape))
    spots = []
    for shift in (0, 1):
        where = [jax.random.randint(jax.random.fold_in(stream_key, axis), (), 0, length) for axis, length in enumerate(drawn.shape)]
        where[longest] = (where[longest] + shift) % drawn.shape[longest]
        spots.append(tuple(where))
    return drawn.at[spots[0]].set(least).at[spots[1]].set(top_value)


def levels(rng, dims, cuts, least, largest):
    level = 1.0
    for dim, blocks in cuts:
        heights = jax.random.uniform(jax.random.fold_in(jax.random.fold_in(rng, 6), dim), (blocks,), jnp.float32, least / len(cuts), largest / len(cuts))
        level = level * jnp.repeat(jnp.exp(heights), dims[dim] // blocks).reshape((-1,) + (1,) * (len(dims) - 1 - dim))
    return level


def gaussian(own_key, dims, spread, bound, cuts=(), kind=jnp.bfloat16):
    gain = levels(own_key, dims, cuts, -0.22, 0.18) if cuts else 1.0
    values = jax.random.normal(own_key, dims, jnp.float32) * spread * gain
    return jnp.minimum(jnp.maximum(values, -bound), bound).astype(kind)


def setup_inputs(seed: int = 0) -> dict:
    streams_of = jax.random.split(jax.random.key(seed), 7)
    return {
        "blocks": gaussian(streams_of[0], (N_GRP, MAX_BLOCKS, ROWS, BLK, BLK), 1.0, 6.0, ((0, 4), (2, 8))),
        "coords": touch_ends(jax.random.randint(streams_of[1], (N_GRP, N_SLAB, MAX_BLOCKS, 2), 0, NBLK), jax.random.fold_in(streams_of[1], 1), 0, NBLK - 1).astype(jnp.int32),
        "counts": draw_counts(jax.random.fold_in(streams_of[6], 71), 0),
        "omega1": gaussian(streams_of[3], (ROWS, RANK), ROWS ** -0.5, 0.5),
        "omega2": gaussian(streams_of[4], (NBLK * BLK, RANK), BLK ** -0.5, 0.5),
        "omega3": gaussian(streams_of[5], (NBLK * BLK, RANK), (BLK * 16) ** -0.5, 0.125),
    }


def contract(running, one_block, coordinate, omega2, omega3):
    block_edge = one_block.shape[-1]
    third_rows = lax.dynamic_slice_in_dim(omega3, (coordinate[1] * block_edge).astype(jnp.int32), block_edge, 0)
    second_rows = lax.dynamic_slice_in_dim(omega2, (coordinate[0] * block_edge).astype(jnp.int32), block_edge, 0)
    after_third = jnp.einsum("iab,bs->ias", one_block.astype(jnp.float32), third_rows.astype(jnp.float32)).astype(jnp.bfloat16)
    return running + jnp.einsum("ias,ar->irs", after_third.astype(jnp.float32), second_rows.astype(jnp.float32))


def reference(blocks, coords, counts, omega1, omega2, omega3):
    def slab_sketch(slab_index):
        running = jnp.zeros((ROWS_DEV, RANK, RANK), jnp.float32)
        for group_index in range(N_GRP):
            def add_slot(position, running, group_index=group_index):
                position = position.astype(jnp.int32)
                one_block = lax.dynamic_slice(blocks, (jnp.int32(group_index), position, (slab_index * ROWS_DEV).astype(jnp.int32), jnp.int32(0), jnp.int32(0)), (1, 1, ROWS_DEV, BLK, BLK))[0, 0]
                coordinate = lax.dynamic_slice(coords, (jnp.int32(group_index), slab_index.astype(jnp.int32), position, jnp.int32(0)), (1, 1, 1, 2))[0, 0, 0]
                return contract(running, one_block, coordinate, omega2, omega3)
            running = lax.fori_loop(jnp.int32(0), counts[group_index, slab_index].astype(jnp.int32), add_slot, running)
        return running

    sketch = lax.map(slab_sketch, jnp.arange(N_SLAB, dtype=jnp.int32))
    folded = sketch.reshape(ROWS, RANK, RANK).astype(jnp.bfloat16)
    return jnp.einsum("ir,ipq->rpq", omega1.astype(jnp.float32), folded.astype(jnp.float32))
```

```python
import functools

import jax
import jax.numpy as jnp
from jax import lax
from jax.experimental import pallas as pl
from jax.experimental.pallas import tpu as pltpu
from jax.sharding import PartitionSpec as P

MESH = pl.DeviceIdType.MESH
LANES = 128


def exchange_kernel(
    n_slab, chunk, blocks, meta, omega2, omega3, out,
    held, metas, places, second, third, second_cat, after_cat, folded,
    load_sem, own_sem, meta_send, meta_recv, block_send, block_recv, fold_send, fold_recv,
):
    slab, grp = lax.axis_index("slab"), lax.axis_index("grp")
    n_slots, depth, edge = held.shape[1], held.shape[2], held.shape[3]
    n_chunks = depth // chunk
    rank = second.shape[2]
    share = rank // n_slab
    partner = (grp, grp + 1 - 2 * lax.rem(grp, 2), lax.rem(grp + 2, 4), 3 - grp)

    def other_slab(distance):
        return lax.rem(slab + distance, n_slab)

    barrier = pltpu.get_barrier_semaphore()
    for relation in (1, 2, 3):
        pl.semaphore_signal(barrier, inc=1, device_id=(slab, partner[relation]), device_id_type=MESH)

    def greet(distance, carry):
        pl.semaphore_signal(barrier, inc=1, device_id=(other_slab(distance), grp), device_id_type=MESH)
        return carry

    lax.fori_loop(1, n_slab, greet, 0)

    cols = pl.ds(pl.multiple_of(grp * LANES, LANES), LANES)
    loads = [
        pltpu.make_async_copy(meta, metas.at[0], load_sem.at[0]),
        pltpu.make_async_copy(omega2, second, load_sem.at[1]),
        pltpu.make_async_copy(omega3.at[:, :, cols], third, load_sem.at[2]),
        pltpu.make_async_copy(blocks, held.at[0], load_sem.at[3]),
    ]
    for load in loads:
        load.start()
    pl.semaphore_wait(barrier, 3 + n_slab - 1)

    def meta_copy(relation):
        return pltpu.make_async_remote_copy(
            src_ref=meta, dst_ref=metas.at[relation],
            send_sem=meta_send.at[relation], recv_sem=meta_recv.at[relation],
            device_id=(slab, partner[relation]), device_id_type=MESH,
        )

    def block_copy(relation, position):
        rows = pl.ds(position * chunk, chunk)
        source = held.at[2, :, rows] if relation == 3 else blocks.at[:, rows]
        target = partner[1] if relation == 3 else partner[relation]
        return pltpu.make_async_remote_copy(
            src_ref=source, dst_ref=held.at[relation, :, rows],
            send_sem=block_send.at[relation, position], recv_sem=block_recv.at[relation, position],
            device_id=(slab, target), device_id_type=MESH,
        )

    for relation in (1, 2, 3):
        meta_copy(relation).start()

    def send_blocks(position, carry):
        block_copy(2, position).start()
        block_copy(1, position).start()
        return carry

    lax.fori_loop(0, n_chunks, send_blocks, 0)

    for relation in (1, 2, 3):
        meta_copy(relation).wait()
    for load in loads:
        load.wait()
    to_scalars = pltpu.make_async_copy(metas, places, load_sem.at[0])
    to_scalars.start()
    to_scalars.wait()

    for relation in range(4):
        for slot in range(n_slots):
            live = places[relation, 2, slot].astype(jnp.float32)
            rows = second[places[relation, 1, slot]].astype(jnp.float32) * live
            place = (relation * n_slots + slot) * edge
            second_cat[:, place:place + edge] = rows.T.astype(jnp.bfloat16)

    def contract_third(relation, position):
        for slot in range(n_slots):
            part = held[relation, slot, pl.ds(position * chunk, chunk)].reshape(chunk * edge, edge)
            product = jnp.dot(part, third[places[relation, 0, slot]], preferred_element_type=jnp.float32)
            product = product.astype(jnp.bfloat16)
            place = (relation * n_slots + slot) * edge
            for row in range(chunk):
                after_cat[place:place + edge, row * LANES:(row + 1) * LANES] = product[row * edge:(row + 1) * edge]

    def fold_copy(distance, position):
        rows = pl.ds(position * chunk, chunk)
        target = other_slab(distance)
        return pltpu.make_async_remote_copy(
            src_ref=folded.at[target, rows], dst_ref=out.at[slab, rows],
            send_sem=fold_send.at[target], recv_sem=fold_recv.at[slab],
            device_id=(target, grp), device_id_type=MESH,
        )

    def step(position, carry):
        block_copy(2, position).wait_recv()
        block_copy(3, position).start()
        contract_third(0, position)
        contract_third(2, position)
        block_copy(1, position).wait_recv()
        contract_third(1, position)
        block_copy(3, position).wait_recv()
        contract_third(3, position)
        summed = jnp.dot(second_cat[...], after_cat[...], preferred_element_type=jnp.float32)
        for target in range(n_slab):
            for row in range(chunk):
                piece = summed[target * share:(target + 1) * share, row * LANES:(row + 1) * LANES]
                folded[target, position * chunk + row] = piece.astype(jnp.bfloat16)

        def send_fold(turn, inner):
            fold_copy(lax.rem(n_slab // 2 - 1 + turn, n_slab - 1) + 1, position).start()
            return inner

        return lax.fori_loop(0, n_slab - 1, send_fold, carry)

    lax.fori_loop(0, n_chunks, step, 0)

    own = pltpu.make_async_copy(folded.at[slab], out.at[slab], own_sem)
    own.start()

    def finish_blocks(position, carry):
        for relation in (1, 2, 3):
            block_copy(relation, position).wait_send()
        return carry

    lax.fori_loop(0, n_chunks, finish_blocks, 0)

    def finish_fold(distance, carry):
        other = other_slab(distance)
        whole = pltpu.make_async_remote_copy(
            src_ref=folded.at[other], dst_ref=out.at[other],
            send_sem=fold_send.at[other], recv_sem=fold_recv.at[other],
            device_id=(other, grp), device_id_type=MESH,
        )
        whole.wait()
        return carry

    lax.fori_loop(1, n_slab, finish_fold, 0)
    own.wait()


def exchange(blocks, meta, omega2, omega3, n_slab, chunk):
    n_slots, depth, edge, _ = blocks.shape
    rank = omega2.shape[2]
    n_chunks = depth // chunk
    live_rows = 4 * n_slots * edge
    anywhere = pl.BlockSpec(memory_space=pl.ANY)
    dma = pltpu.SemaphoreType.DMA
    return pl.pallas_call(
        functools.partial(exchange_kernel, n_slab, chunk),
        out_shape=jax.ShapeDtypeStruct((n_slab, depth, rank // n_slab, LANES), jnp.bfloat16),
        in_specs=[anywhere] * 4,
        out_specs=anywhere,
        scratch_shapes=[
            pltpu.VMEM((4, n_slots, depth, edge, edge), jnp.bfloat16),
            pltpu.VMEM((4, 8, LANES), jnp.int32),
            pltpu.SMEM((4, 8, LANES), jnp.int32),
            pltpu.VMEM(omega2.shape, jnp.bfloat16),
            pltpu.VMEM((*omega3.shape[:2], LANES), jnp.bfloat16),
            pltpu.VMEM((rank, live_rows), jnp.bfloat16),
            pltpu.VMEM((live_rows, chunk * LANES), jnp.bfloat16),
            pltpu.VMEM((n_slab, depth, rank // n_slab, LANES), jnp.bfloat16),
            dma((4,)),
            dma,
            dma((4,)),
            dma((4,)),
            dma((4, n_chunks)),
            dma((4, n_chunks)),
            dma((n_slab,)),
            dma((n_slab,)),
        ],
        compiler_params=pltpu.CompilerParams(
            collective_id=0, has_side_effects=True, vmem_limit_bytes=40 * 2**20
        ),
        cost_estimate=pl.CostEstimate(
            flops=2 * live_rows * depth * LANES * (edge + rank),
            bytes_accessed=24 * 2**20, transcendentals=0,
        ),
        name="exchange",
    )(blocks, meta, omega2, omega3)


def core_kernel(received, omega1, out, wide, by_row, weights):
    n_slab, depth, share, _ = received.shape
    rows, rank = omega1.shape

    @pl.when(pl.program_id(0) == 0)
    def _():
        weights[...] = omega1[...].astype(jnp.float32).T.astype(jnp.bfloat16)

    def spread(slab, carry):
        for row in range(depth):
            wide[pl.ds(slab * depth + row, share, stride=rows), :] = received[slab, row].astype(jnp.float32)
        return carry

    lax.fori_loop(0, n_slab, spread, 0)
    for column in range(share):
        by_row[:, column * LANES:(column + 1) * LANES] = wide[
            column * rows:(column + 1) * rows, :
        ].astype(jnp.bfloat16)
    flat = out.reshape(rank * share, LANES)
    for column in range(0, share, 2):
        product = jnp.dot(
            weights[...], by_row[:, column * LANES:(column + 2) * LANES], preferred_element_type=jnp.float32
        )
        for side in range(2):
            flat[pl.ds(column + side, rank, stride=share), :] = product[:, side * LANES:(side + 1) * LANES]


def core(received, omega1):
    n_slab, depth, share, _ = received.shape
    rows, rank = omega1.shape
    tile = min(16, share)
    return pl.pallas_call(
        core_kernel,
        grid=(share // tile,),
        out_shape=jax.ShapeDtypeStruct((rank, share, LANES), jnp.float32),
        in_specs=[
            pl.BlockSpec((n_slab, depth, tile, LANES), lambda t: (0, 0, t, 0)),
            pl.BlockSpec((rows, rank), lambda t: (0, 0)),
        ],
        out_specs=pl.BlockSpec((rank, tile, LANES), lambda t: (0, t, 0)),
        scratch_shapes=[
            pltpu.VMEM((tile * rows, LANES), jnp.float32),
            pltpu.VMEM((rows, tile * LANES), jnp.bfloat16),
            pltpu.VMEM((rank, rows), jnp.bfloat16),
        ],
        compiler_params=pltpu.CompilerParams(vmem_limit_bytes=40 * 2**20),
        cost_estimate=pl.CostEstimate(
            flops=2 * rank * rows * share * LANES,
            bytes_accessed=rank * share * LANES * 4, transcendentals=0,
        ),
        name="core",
    )(received, omega1)


def local(n_slab, blocks, coords, counts, omega1, omega2, omega3):
    own_blocks = blocks[0]
    n_slots, depth, edge, _ = own_blocks.shape
    corners = coords[0, 0]
    omega2 = omega2.reshape(-1, edge, omega2.shape[1])
    omega3 = omega3.reshape(-1, edge, omega3.shape[1])
    live = (jnp.arange(n_slots) < counts[0, 0]).astype(jnp.int32)
    meta = jnp.stack([corners[:, 1], corners[:, 0], live])
    meta = jnp.pad(meta, ((0, 5), (0, LANES - n_slots)))
    received = exchange(own_blocks, meta, omega2, omega3, n_slab, 2)
    return core(received, omega1)


def solution(mesh):
    in_specs = (
        P("grp", None, "slab", None, None),
        P("grp", "slab", None, None),
        P("grp", "slab"),
        P(),
        P(),
        P(),
    )
    out_specs = P(None, "slab", "grp")
    body = functools.partial(local, mesh.shape["slab"])
    return jax.shard_map(body, mesh=mesh, in_specs=in_specs, out_specs=out_specs, check_vma=False)
```

```python
import functools

import jax
import jax.numpy as jnp
from jax import lax
from jax.experimental import pallas as pl
from jax.experimental.pallas import tpu as pltpu
from jax.sharding import PartitionSpec as P

MESH = pl.DeviceIdType.MESH
LANES = 128


def exchange_kernel(
    n_slab, chunk, blocks, meta, omega2, omega3, out,
    held, metas, places, second, third, second_cat, after_cat, folded,
    load_sem, own_sem, meta_send, meta_recv, block_send, block_recv, fold_send, fold_recv,
):
    slab, grp = lax.axis_index("slab"), lax.axis_index("grp")
    n_slots, depth, edge = held.shape[1], held.shape[2], held.shape[3]
    n_chunks = depth // chunk
    rank = second.shape[2]
    share = rank // n_slab
    partner = (grp, grp + 1 - 2 * lax.rem(grp, 2), lax.rem(grp + 2, 4), 3 - grp)

    def other_slab(distance):
        return lax.rem(slab + distance, n_slab)

    barrier = pltpu.get_barrier_semaphore()
    for relation in (1, 2, 3):
        pl.semaphore_signal(barrier, inc=1, device_id=(slab, partner[relation]), device_id_type=MESH)

    def greet(distance, carry):
        pl.semaphore_signal(barrier, inc=1, device_id=(other_slab(distance), grp), device_id_type=MESH)
        return carry

    lax.fori_loop(1, n_slab, greet, 0)

    cols = pl.ds(pl.multiple_of(grp * LANES, LANES), LANES)
    loads = [
        pltpu.make_async_copy(meta, metas.at[0], load_sem.at[0]),
        pltpu.make_async_copy(omega2, second, load_sem.at[1]),
        pltpu.make_async_copy(omega3.at[:, :, cols], third, load_sem.at[2]),
        pltpu.make_async_copy(blocks, held.at[0], load_sem.at[3]),
    ]
    for load in loads:
        load.start()
    pl.semaphore_wait(barrier, 3 + n_slab - 1)

    def meta_copy(relation):
        return pltpu.make_async_remote_copy(
            src_ref=meta, dst_ref=metas.at[relation],
            send_sem=meta_send.at[relation], recv_sem=meta_recv.at[relation],
            device_id=(slab, partner[relation]), device_id_type=MESH,
        )

    def block_copy(relation, position):
        rows = pl.ds(position * chunk, chunk)
        source = held.at[2, :, rows] if relation == 3 else blocks.at[:, rows]
        target = partner[1] if relation == 3 else partner[relation]
        return pltpu.make_async_remote_copy(
            src_ref=source, dst_ref=held.at[relation, :, rows],
            send_sem=block_send.at[relation, position], recv_sem=block_recv.at[relation, position],
            device_id=(slab, target), device_id_type=MESH,
        )

    for relation in (1, 2, 3):
        meta_copy(relation).start()

    def send_blocks(position, carry):
        block_copy(2, position).start()
        block_copy(1, position).start()
        return carry

    lax.fori_loop(0, n_chunks, send_blocks, 0)

    for relation in (1, 2, 3):
        meta_copy(relation).wait()
    for load in loads:
        load.wait()
    to_scalars = pltpu.make_async_copy(metas, places, load_sem.at[0])
    to_scalars.start()
    to_scalars.wait()

    for relation in range(4):
        for slot in range(n_slots):
            live = places[relation, 2, slot].astype(jnp.float32)
            rows = second[places[relation, 1, slot]].astype(jnp.float32) * live
            place = (relation * n_slots + slot) * edge
            second_cat[:, place:place + edge] = rows.astype(jnp.bfloat16).T

    def contract_third(relation, position):
        for slot in range(n_slots):
            part = held[relation, slot, pl.ds(position * chunk, chunk)].reshape(chunk * edge, edge)
            product = jnp.dot(part, third[places[relation, 0, slot]], preferred_element_type=jnp.float32)
            product = product.astype(jnp.bfloat16)
            place = (relation * n_slots + slot) * edge
            for row in range(chunk):
                after_cat[place:place + edge, row * LANES:(row + 1) * LANES] = product[row * edge:(row + 1) * edge]

    def fold_copy(distance, position):
        rows = pl.ds(position * chunk, chunk)
        target = other_slab(distance)
        return pltpu.make_async_remote_copy(
            src_ref=folded.at[target, rows], dst_ref=out.at[slab, rows],
            send_sem=fold_send.at[target], recv_sem=fold_recv.at[slab],
            device_id=(target, grp), device_id_type=MESH,
        )

    def step(position, carry):
        block_copy(2, position).wait_recv()
        block_copy(3, position).start()
        contract_third(0, position)
        contract_third(2, position)
        block_copy(1, position).wait_recv()
        contract_third(1, position)
        block_copy(3, position).wait_recv()
        contract_third(3, position)
        summed = jnp.dot(second_cat[...], after_cat[...], preferred_element_type=jnp.float32)
        for target in range(n_slab):
            for row in range(chunk):
                piece = summed[target * share:(target + 1) * share, row * LANES:(row + 1) * LANES]
                folded[target, position * chunk + row] = piece.astype(jnp.bfloat16)

        def send_fold(turn, inner):
            fold_copy(lax.rem(n_slab // 2 - 1 + turn, n_slab - 1) + 1, position).start()
            return inner

        return lax.fori_loop(0, n_slab - 1, send_fold, carry)

    lax.fori_loop(0, n_chunks, step, 0)

    own = pltpu.make_async_copy(folded.at[slab], out.at[slab], own_sem)
    own.start()

    def finish_blocks(position, carry):
        for relation in (1, 2, 3):
            block_copy(relation, position).wait_send()
        return carry

    lax.fori_loop(0, n_chunks, finish_blocks, 0)

    def finish_fold(distance, carry):
        other = other_slab(distance)
        whole = pltpu.make_async_remote_copy(
            src_ref=folded.at[other], dst_ref=out.at[other],
            send_sem=fold_send.at[other], recv_sem=fold_recv.at[other],
            device_id=(other, grp), device_id_type=MESH,
        )
        whole.wait()
        return carry

    lax.fori_loop(1, n_slab, finish_fold, 0)
    own.wait()


def exchange(blocks, meta, omega2, omega3, n_slab, chunk):
    n_slots, depth, edge, _ = blocks.shape
    rank = omega2.shape[2]
    n_chunks = depth // chunk
    live_rows = 4 * n_slots * edge
    anywhere = pl.BlockSpec(memory_space=pl.ANY)
    dma = pltpu.SemaphoreType.DMA
    return pl.pallas_call(
        functools.partial(exchange_kernel, n_slab, chunk),
        out_shape=jax.ShapeDtypeStruct((n_slab, depth, rank // n_slab, LANES), jnp.bfloat16),
        in_specs=[anywhere] * 4,
        out_specs=anywhere,
        scratch_shapes=[
            pltpu.VMEM((4, n_slots, depth, edge, edge), jnp.bfloat16),
            pltpu.VMEM((4, 8, LANES), jnp.int32),
            pltpu.SMEM((4, 8, LANES), jnp.int32),
            pltpu.VMEM(omega2.shape, jnp.bfloat16),
            pltpu.VMEM((*omega3.shape[:2], LANES), jnp.bfloat16),
            pltpu.VMEM((rank, live_rows), jnp.bfloat16),
            pltpu.VMEM((live_rows, chunk * LANES), jnp.bfloat16),
            pltpu.VMEM((n_slab, depth, rank // n_slab, LANES), jnp.bfloat16),
            dma((4,)),
            dma,
            dma((4,)),
            dma((4,)),
            dma((4, n_chunks)),
            dma((4, n_chunks)),
            dma((n_slab,)),
            dma((n_slab,)),
        ],
        compiler_params=pltpu.CompilerParams(
            collective_id=0, has_side_effects=True, vmem_limit_bytes=62 * 2**20
        ),
        cost_estimate=pl.CostEstimate(
            flops=2 * live_rows * depth * LANES * (edge + rank),
            bytes_accessed=24 * 2**20, transcendentals=0,
        ),
        name="exchange",
    )(blocks, meta, omega2, omega3)


def core_kernel(received, omega1, out, by_row, weights, swap):
    n_slab, depth, share, _ = received.shape
    rows, rank = omega1.shape
    size = depth * share

    @pl.when(pl.program_id(0) == 0)
    def _():
        weights[...] = omega1[...].astype(jnp.float32).T.astype(jnp.bfloat16)
        to_place = lax.broadcasted_iota(jnp.int32, (size, size), 0)
        from_place = lax.broadcasted_iota(jnp.int32, (size, size), 1)
        wanted = lax.rem(to_place, depth) * share + lax.div(to_place, depth)
        swap[...] = (from_place == wanted).astype(jnp.float32).astype(jnp.bfloat16)

    for slab in range(n_slab):
        natural = received[slab]
        if share % 16:
            natural = natural.astype(jnp.float32)
        natural = natural.reshape(size, LANES).astype(jnp.bfloat16)
        moved = jnp.dot(swap[...], natural, preferred_element_type=jnp.float32).astype(jnp.bfloat16)
        for column in range(share):
            by_row[slab * depth:(slab + 1) * depth, column * LANES:(column + 1) * LANES] = moved[
                column * depth:(column + 1) * depth
            ]
    flat = out.reshape(rank * share, LANES)
    for column in range(0, share, 2):
        product = jnp.dot(
            weights[...], by_row[:, column * LANES:(column + 2) * LANES], preferred_element_type=jnp.float32
        )
        for side in range(2):
            flat[pl.ds(column + side, rank, stride=share), :] = product[:, side * LANES:(side + 1) * LANES]


def core(received, omega1):
    n_slab, depth, share, _ = received.shape
    rows, rank = omega1.shape
    tile = min(16, share)
    return pl.pallas_call(
        core_kernel,
        grid=(share // tile,),
        out_shape=jax.ShapeDtypeStruct((rank, share, LANES), jnp.float32),
        in_specs=[
            pl.BlockSpec((n_slab, depth, tile, LANES), lambda t: (0, 0, t, 0)),
            pl.BlockSpec((rows, rank), lambda t: (0, 0)),
        ],
        out_specs=pl.BlockSpec((rank, tile, LANES), lambda t: (0, t, 0)),
        scratch_shapes=[
            pltpu.VMEM((rows, tile * LANES), jnp.bfloat16),
            pltpu.VMEM((rank, rows), jnp.bfloat16),
            pltpu.VMEM((depth * tile, depth * tile), jnp.bfloat16),
        ],
        compiler_params=pltpu.CompilerParams(vmem_limit_bytes=40 * 2**20),
        cost_estimate=pl.CostEstimate(
            flops=2 * rank * rows * share * LANES,
            bytes_accessed=rank * share * LANES * 4, transcendentals=0,
        ),
        name="core",
    )(received, omega1)


def local(n_slab, blocks, coords, counts, omega1, omega2, omega3):
    own_blocks = blocks[0]
    n_slots, depth, edge, _ = own_blocks.shape
    corners = coords[0, 0]
    omega2 = omega2.reshape(-1, edge, omega2.shape[1])
    omega3 = omega3.reshape(-1, edge, omega3.shape[1])
    live = (jnp.arange(n_slots) < counts[0, 0]).astype(jnp.int32)
    meta = jnp.stack([corners[:, 1], corners[:, 0], live])
    meta = jnp.pad(meta, ((0, 5), (0, LANES - n_slots)))
    received = exchange(own_blocks, meta, omega2, omega3, n_slab, 1)
    return core(received, omega1)


def solution(mesh):
    in_specs = (
        P("grp", None, "slab", None, None),
        P("grp", "slab", None, None),
        P("grp", "slab"),
        P(),
        P(),
        P(),
    )
    out_specs = P(None, "slab", "grp")
    body = functools.partial(local, mesh.shape["slab"])
    return jax.shard_map(body, mesh=mesh, in_specs=in_specs, out_specs=out_specs, check_vma=False)
```

```python
import functools

import jax
import jax.numpy as jnp
from jax import lax
from jax.experimental import pallas as pl
from jax.experimental.pallas import tpu as pltpu
from jax.sharding import PartitionSpec as P

MESH = pl.DeviceIdType.MESH
LANES = 128


def exchange_kernel(
    n_slab, chunk, blocks, meta, omega2, omega3, out,
    held, metas, places, second, third, second_cat, after_cat, folded,
    load_sem, own_sem, meta_send, meta_recv, block_send, block_recv, fold_send, fold_recv,
):
    slab, grp = lax.axis_index("slab"), lax.axis_index("grp")
    n_slots, depth, edge = held.shape[1], held.shape[2], held.shape[3]
    n_chunks = depth // chunk
    rank = second.shape[2]
    share = rank // n_slab
    partner = (grp, grp + 1 - 2 * lax.rem(grp, 2), lax.rem(grp + 2, 4), 3 - grp)

    def other_slab(distance):
        return lax.rem(slab + distance, n_slab)

    barrier = pltpu.get_barrier_semaphore()
    for relation in (1, 2, 3):
        pl.semaphore_signal(barrier, inc=1, device_id=(slab, partner[relation]), device_id_type=MESH)

    def greet(distance, carry):
        pl.semaphore_signal(barrier, inc=1, device_id=(other_slab(distance), grp), device_id_type=MESH)
        return carry

    lax.fori_loop(1, n_slab, greet, 0)

    cols = pl.ds(pl.multiple_of(grp * LANES, LANES), LANES)
    loads = [
        pltpu.make_async_copy(meta, metas.at[0], load_sem.at[0]),
        pltpu.make_async_copy(omega2, second, load_sem.at[1]),
        pltpu.make_async_copy(omega3.at[:, :, cols], third, load_sem.at[2]),
        pltpu.make_async_copy(blocks, held.at[0], load_sem.at[3]),
    ]
    for load in loads:
        load.start()
    pl.semaphore_wait(barrier, 3 + n_slab - 1)

    def meta_copy(relation):
        return pltpu.make_async_remote_copy(
            src_ref=meta, dst_ref=metas.at[relation],
            send_sem=meta_send.at[relation], recv_sem=meta_recv.at[relation],
            device_id=(slab, partner[relation]), device_id_type=MESH,
        )

    def block_copy(relation, position):
        rows = pl.ds(position * chunk, chunk)
        source = held.at[2, :, rows] if relation == 3 else blocks.at[:, rows]
        target = partner[1] if relation == 3 else partner[relation]
        return pltpu.make_async_remote_copy(
            src_ref=source, dst_ref=held.at[relation, :, rows],
            send_sem=block_send.at[relation, position], recv_sem=block_recv.at[relation, position],
            device_id=(slab, target), device_id_type=MESH,
        )

    for relation in (1, 2, 3):
        meta_copy(relation).start()

    def send_blocks(position, carry):
        block_copy(2, position).start()
        block_copy(1, position).start()
        return carry

    lax.fori_loop(0, n_chunks, send_blocks, 0)

    block_copy(2, 0).wait_recv()
    block_copy(3, 0).start()
    for relation in (1, 2, 3):
        meta_copy(relation).wait()
    for load in loads:
        load.wait()
    to_scalars = pltpu.make_async_copy(metas, places, load_sem.at[0])
    to_scalars.start()
    to_scalars.wait()

    for relation in range(4):
        for slot in range(n_slots):
            live = places[relation, 2, slot].astype(jnp.float32)
            rows = second[places[relation, 0, slot]].astype(jnp.float32) * live
            place = (relation * n_slots + slot) * edge
            second_cat[:, place:place + edge] = rows.astype(jnp.bfloat16).T

    def contract_third(relation, position):
        for slot in range(n_slots):
            part = held[relation, slot, pl.ds(position * chunk, chunk)].reshape(chunk * edge, edge)
            product = jnp.dot(part, third[places[relation, 1, slot]], preferred_element_type=jnp.float32)
            product = product.astype(jnp.bfloat16)
            place = (relation * n_slots + slot) * edge
            for row in range(chunk):
                after_cat[place:place + edge, row * LANES:(row + 1) * LANES] = product[row * edge:(row + 1) * edge]

    def fold_copy(distance, position):
        rows = pl.ds(position * chunk, chunk)
        target = other_slab(distance)
        return pltpu.make_async_remote_copy(
            src_ref=folded.at[target, rows], dst_ref=out.at[slab, rows],
            send_sem=fold_send.at[target], recv_sem=fold_recv.at[slab],
            device_id=(target, grp), device_id_type=MESH,
        )

    def step(position, carry):
        @pl.when(position > 0)
        def _():
            block_copy(2, position).wait_recv()
            block_copy(3, position).start()

        contract_third(0, position)
        contract_third(2, position)
        block_copy(1, position).wait_recv()
        contract_third(1, position)
        block_copy(3, position).wait_recv()
        contract_third(3, position)
        summed = jnp.dot(second_cat[...], after_cat[...], preferred_element_type=jnp.float32)
        for target in range(n_slab):
            for row in range(chunk):
                piece = summed[target * share:(target + 1) * share, row * LANES:(row + 1) * LANES]
                folded[target, position * chunk + row] = piece.astype(jnp.bfloat16)

        def send_fold(turn, inner):
            fold_copy(lax.rem(n_slab // 2 - 1 + turn, n_slab - 1) + 1, position).start()
            return inner

        return lax.fori_loop(0, n_slab - 1, send_fold, carry)

    lax.fori_loop(0, n_chunks, step, 0)

    own = pltpu.make_async_copy(folded.at[slab], out.at[slab], own_sem)
    own.start()

    def finish_blocks(position, carry):
        for relation in (1, 2, 3):
            block_copy(relation, position).wait_send()
        return carry

    lax.fori_loop(0, n_chunks, finish_blocks, 0)

    def finish_fold(distance, carry):
        other = other_slab(distance)
        whole = pltpu.make_async_remote_copy(
            src_ref=folded.at[other], dst_ref=out.at[other],
            send_sem=fold_send.at[other], recv_sem=fold_recv.at[other],
            device_id=(other, grp), device_id_type=MESH,
        )
        whole.wait()
        return carry

    lax.fori_loop(1, n_slab, finish_fold, 0)
    own.wait()


def exchange(blocks, meta, omega2, omega3, n_slab, chunk):
    n_slots, depth, edge, _ = blocks.shape
    rank = omega2.shape[2]
    n_chunks = depth // chunk
    live_rows = 4 * n_slots * edge
    anywhere = pl.BlockSpec(memory_space=pl.ANY)
    dma = pltpu.SemaphoreType.DMA
    return pl.pallas_call(
        functools.partial(exchange_kernel, n_slab, chunk),
        out_shape=jax.ShapeDtypeStruct((n_slab, depth, rank // n_slab, LANES), jnp.bfloat16),
        in_specs=[anywhere] * 4,
        out_specs=anywhere,
        scratch_shapes=[
            pltpu.VMEM((4, n_slots, depth, edge, edge), jnp.bfloat16),
            pltpu.VMEM((4, 8, LANES), jnp.int32),
            pltpu.SMEM((4, 8, LANES), jnp.int32),
            pltpu.VMEM(omega2.shape, jnp.bfloat16),
            pltpu.VMEM((*omega3.shape[:2], LANES), jnp.bfloat16),
            pltpu.VMEM((rank, live_rows), jnp.bfloat16),
            pltpu.VMEM((live_rows, chunk * LANES), jnp.bfloat16),
            pltpu.VMEM((n_slab, depth, rank // n_slab, LANES), jnp.bfloat16),
            dma((4,)),
            dma,
            dma((4,)),
            dma((4,)),
            dma((4, n_chunks)),
            dma((4, n_chunks)),
            dma((n_slab,)),
            dma((n_slab,)),
        ],
        compiler_params=pltpu.CompilerParams(
            collective_id=0, has_side_effects=True, vmem_limit_bytes=62 * 2**20
        ),
        cost_estimate=pl.CostEstimate(
            flops=2 * live_rows * depth * LANES * (edge + rank),
            bytes_accessed=24 * 2**20, transcendentals=0,
        ),
        name="exchange",
    )(blocks, meta, omega2, omega3)


def core_kernel(received, omega1, out, by_row, weights, swap, staged, sems):
    n_slab, depth, share, _ = received.shape
    rows, rank = omega1.shape
    size = depth * share
    step, steps = pl.program_id(0), pl.num_programs(0)
    part = staged.shape[2]

    def store(turn, half):
        columns = pl.ds(pl.multiple_of(turn * share + half * part, part), part)
        return pltpu.make_async_copy(staged.at[half], out.at[:, columns, :], sems.at[half])

    @pl.when(step == 0)
    def _():
        weights[...] = omega1[...].astype(jnp.float32).T.astype(jnp.bfloat16)
        to_place = lax.broadcasted_iota(jnp.int32, (size, size), 0)
        from_place = lax.broadcasted_iota(jnp.int32, (size, size), 1)
        wanted = lax.rem(to_place, depth) * share + lax.div(to_place, depth)
        swap[...] = (from_place == wanted).astype(jnp.float32).astype(jnp.bfloat16)

    for slab in range(n_slab):
        natural = received[slab]
        if share % 16:
            natural = natural.astype(jnp.float32)
        natural = natural.reshape(size, LANES).astype(jnp.bfloat16)
        moved = jnp.dot(swap[...], natural, preferred_element_type=jnp.float32).astype(jnp.bfloat16)
        for column in range(share):
            by_row[slab * depth:(slab + 1) * depth, column * LANES:(column + 1) * LANES] = moved[
                column * depth:(column + 1) * depth
            ]
    flat = staged.reshape(share * rank, LANES)
    for half in range(share // part):
        @pl.when(step > 0)
        def _():
            store(step - 1, half).wait()

        for column in range(0, part, 2):
            place = (half * part + column) * LANES
            product = jnp.dot(
                weights[...], by_row[:, place:place + 2 * LANES], preferred_element_type=jnp.float32
            )
            for side in range(2):
                spots = pl.ds(half * rank * part + column + side, rank, stride=part)
                flat[spots, :] = product[:, side * LANES:(side + 1) * LANES]
        store(step, half).start()

    @pl.when(step == steps - 1)
    def _():
        for half in range(share // part):
            store(step, half).wait()


def core(received, omega1):
    n_slab, depth, share, _ = received.shape
    rows, rank = omega1.shape
    tile, part = min(16, share), min(8, share)
    return pl.pallas_call(
        core_kernel,
        grid=(share // tile,),
        out_shape=jax.ShapeDtypeStruct((rank, share, LANES), jnp.float32),
        in_specs=[
            pl.BlockSpec((n_slab, depth, tile, LANES), lambda t: (0, 0, t, 0)),
            pl.BlockSpec((rows, rank), lambda t: (0, 0)),
        ],
        out_specs=pl.BlockSpec(memory_space=pl.ANY),
        scratch_shapes=[
            pltpu.VMEM((rows, tile * LANES), jnp.bfloat16),
            pltpu.VMEM((rank, rows), jnp.bfloat16),
            pltpu.VMEM((depth * tile, depth * tile), jnp.bfloat16),
            pltpu.VMEM((tile // part, rank, part, LANES), jnp.float32),
            pltpu.SemaphoreType.DMA((tile // part,)),
        ],
        compiler_params=pltpu.CompilerParams(vmem_limit_bytes=62 * 2**20),
        cost_estimate=pl.CostEstimate(
            flops=2 * rank * rows * share * LANES,
            bytes_accessed=rank * share * LANES * 4, transcendentals=0,
        ),
        name="core",
    )(received, omega1)


def local(n_slab, blocks, coords, counts, omega1, omega2, omega3):
    own_blocks = blocks[0]
    n_slots, depth, edge, _ = own_blocks.shape
    row = lax.broadcasted_iota(jnp.int32, (8, LANES), 0)
    lane = lax.broadcasted_iota(jnp.int32, (8, LANES), 1)
    corners = jnp.pad(coords[0, 0].T, ((0, 6), (0, LANES - n_slots)))
    meta = jnp.where(row == 2, (lane < counts[0, 0]).astype(jnp.int32), corners)
    omega2 = omega2.reshape(-1, edge, omega2.shape[1])
    omega3 = omega3.reshape(-1, edge, omega3.shape[1])
    received = exchange(own_blocks, meta, omega2, omega3, n_slab, 1)
    return core(received, omega1)


def solution(mesh):
    in_specs = (
        P("grp", None, "slab", None, None),
        P("grp", "slab", None, None),
        P("grp", "slab"),
        P(),
        P(),
        P(),
    )
    out_specs = P(None, "slab", "grp")
    body = functools.partial(local, mesh.shape["slab"])
    return jax.shard_map(body, mesh=mesh, in_specs=in_specs, out_specs=out_specs, check_vma=False)
```

```python
import functools

import jax
import jax.numpy as jnp
from jax import lax
from jax.experimental import pallas as pl
from jax.experimental.pallas import tpu as pltpu
from jax.sharding import PartitionSpec as P

MESH = pl.DeviceIdType.MESH
LANES = 128


def exchange_kernel(
    n_slab, chunk, blocks, meta, omega2, omega3, out,
    held, metas, places, second, third, second_cat, after_cat, folded,
    load_sem, own_sem, meta_send, meta_recv, block_send, block_recv, fold_send, fold_recv,
):
    slab, grp = lax.axis_index("slab"), lax.axis_index("grp")
    n_slots, depth, edge = held.shape[1], held.shape[2], held.shape[3]
    n_chunks = depth // chunk
    rank = second.shape[2]
    share = rank // n_slab
    partner = (grp, grp + 1 - 2 * lax.rem(grp, 2), lax.rem(grp + 2, 4), 3 - grp)

    def other_slab(distance):
        return lax.rem(slab + distance, n_slab)

    barrier = pltpu.get_barrier_semaphore()
    for relation in (1, 2, 3):
        pl.semaphore_signal(barrier, inc=1, device_id=(slab, partner[relation]), device_id_type=MESH)

    def greet(distance, carry):
        pl.semaphore_signal(barrier, inc=1, device_id=(other_slab(distance), grp), device_id_type=MESH)
        return carry

    lax.fori_loop(1, n_slab, greet, 0)

    cols = pl.ds(pl.multiple_of(grp * LANES, LANES), LANES)
    loads = [
        pltpu.make_async_copy(meta, metas.at[0], load_sem.at[0]),
        pltpu.make_async_copy(omega2, second, load_sem.at[1]),
        pltpu.make_async_copy(omega3.at[:, :, cols], third, load_sem.at[2]),
        pltpu.make_async_copy(blocks, held.at[0], load_sem.at[3]),
    ]
    for load in loads:
        load.start()
    pl.semaphore_wait(barrier, 3 + n_slab - 1)

    def meta_copy(relation):
        return pltpu.make_async_remote_copy(
            src_ref=meta, dst_ref=metas.at[relation],
            send_sem=meta_send.at[relation], recv_sem=meta_recv.at[relation],
            device_id=(slab, partner[relation]), device_id_type=MESH,
        )

    def block_copy(relation, position):
        rows = pl.ds(position * chunk, chunk)
        source = held.at[2, :, rows] if relation == 3 else blocks.at[:, rows]
        target = partner[1] if relation == 3 else partner[relation]
        return pltpu.make_async_remote_copy(
            src_ref=source, dst_ref=held.at[relation, :, rows],
            send_sem=block_send.at[relation, position], recv_sem=block_recv.at[relation, position],
            device_id=(slab, target), device_id_type=MESH,
        )

    for relation in (1, 2, 3):
        meta_copy(relation).start()

    def send_blocks(position, carry):
        block_copy(2, position).start()
        return carry

    def send_pair(position, carry):
        block_copy(1, position).start()
        return carry

    lax.fori_loop(0, n_chunks, send_blocks, 0)
    lax.fori_loop(0, n_chunks, send_pair, 0)

    block_copy(2, 0).wait_recv()
    block_copy(3, 0).start()
    for relation in (1, 2, 3):
        meta_copy(relation).wait()
    for load in loads:
        load.wait()
    to_scalars = pltpu.make_async_copy(metas, places, load_sem.at[0])
    to_scalars.start()
    to_scalars.wait()

    for relation in range(4):
        for slot in range(n_slots):
            live = places[relation, 2, slot].astype(jnp.float32)
            rows = second[places[relation, 0, slot]].astype(jnp.float32) * live
            place = (relation * n_slots + slot) * edge
            second_cat[:, place:place + edge] = rows.astype(jnp.bfloat16).T

    def contract_third(relation, position):
        for slot in range(n_slots):
            part = held[relation, slot, pl.ds(position * chunk, chunk)].reshape(chunk * edge, edge)
            product = jnp.dot(part, third[places[relation, 1, slot]], preferred_element_type=jnp.float32)
            product = product.astype(jnp.bfloat16)
            place = (relation * n_slots + slot) * edge
            for row in range(chunk):
                after_cat[place:place + edge, row * LANES:(row + 1) * LANES] = product[row * edge:(row + 1) * edge]

    def fold_copy(distance, position):
        rows = pl.ds(position * chunk, chunk)
        target = other_slab(distance)
        return pltpu.make_async_remote_copy(
            src_ref=folded.at[target, rows], dst_ref=out.at[slab, rows],
            send_sem=fold_send.at[target], recv_sem=fold_recv.at[slab],
            device_id=(target, grp), device_id_type=MESH,
        )

    def step(position, carry):
        @pl.when(position > 0)
        def _():
            block_copy(2, position).wait_recv()
            block_copy(3, position).start()

        contract_third(0, position)
        contract_third(2, position)
        block_copy(1, position).wait_recv()
        contract_third(1, position)
        block_copy(3, position).wait_recv()
        contract_third(3, position)
        summed = jnp.dot(second_cat[...], after_cat[...], preferred_element_type=jnp.float32)
        for target in range(n_slab):
            for row in range(chunk):
                piece = summed[target * share:(target + 1) * share, row * LANES:(row + 1) * LANES]
                folded[target, position * chunk + row] = piece.astype(jnp.bfloat16)

        def send_fold(turn, inner):
            fold_copy(lax.rem(n_slab // 2 - 1 + turn, n_slab - 1) + 1, position).start()
            return inner

        return lax.fori_loop(0, n_slab - 1, send_fold, carry)

    lax.fori_loop(0, n_chunks, step, 0)

    own = pltpu.make_async_copy(folded.at[slab], out.at[slab], own_sem)
    own.start()

    def finish_blocks(position, carry):
        for relation in (1, 2, 3):
            block_copy(relation, position).wait_send()
        return carry

    lax.fori_loop(0, n_chunks, finish_blocks, 0)

    def finish_fold(distance, carry):
        other = other_slab(distance)
        whole = pltpu.make_async_remote_copy(
            src_ref=folded.at[other], dst_ref=out.at[other],
            send_sem=fold_send.at[other], recv_sem=fold_recv.at[other],
            device_id=(other, grp), device_id_type=MESH,
        )
        whole.wait()
        return carry

    lax.fori_loop(1, n_slab, finish_fold, 0)
    own.wait()


def exchange(blocks, meta, omega2, omega3, n_slab, chunk):
    n_slots, depth, edge, _ = blocks.shape
    rank = omega2.shape[2]
    n_chunks = depth // chunk
    live_rows = 4 * n_slots * edge
    anywhere = pl.BlockSpec(memory_space=pl.ANY)
    dma = pltpu.SemaphoreType.DMA
    return pl.pallas_call(
        functools.partial(exchange_kernel, n_slab, chunk),
        out_shape=jax.ShapeDtypeStruct((n_slab, depth, rank // n_slab, LANES), jnp.bfloat16),
        in_specs=[anywhere] * 4,
        out_specs=anywhere,
        scratch_shapes=[
            pltpu.VMEM((4, n_slots, depth, edge, edge), jnp.bfloat16),
            pltpu.VMEM((4, 8, LANES), jnp.int32),
            pltpu.SMEM((4, 8, LANES), jnp.int32),
            pltpu.VMEM(omega2.shape, jnp.bfloat16),
            pltpu.VMEM((*omega3.shape[:2], LANES), jnp.bfloat16),
            pltpu.VMEM((rank, live_rows), jnp.bfloat16),
            pltpu.VMEM((live_rows, chunk * LANES), jnp.bfloat16),
            pltpu.VMEM((n_slab, depth, rank // n_slab, LANES), jnp.bfloat16),
            dma((4,)),
            dma,
            dma((4,)),
            dma((4,)),
            dma((4, n_chunks)),
            dma((4, n_chunks)),
            dma((n_slab,)),
            dma((n_slab,)),
        ],
        compiler_params=pltpu.CompilerParams(
            collective_id=0, has_side_effects=True, vmem_limit_bytes=62 * 2**20
        ),
        cost_estimate=pl.CostEstimate(
            flops=2 * live_rows * depth * LANES * (edge + rank),
            bytes_accessed=24 * 2**20, transcendentals=0,
        ),
        name="exchange",
    )(blocks, meta, omega2, omega3)


def core_kernel(received, omega1, out, by_row, weights, swap, staged, sems):
    n_slab, depth, share, _ = received.shape
    rows, rank = omega1.shape
    size = depth * share
    step, steps = pl.program_id(0), pl.num_programs(0)
    part = staged.shape[2]

    def store(turn, half):
        columns = pl.ds(pl.multiple_of(turn * share + half * part, part), part)
        return pltpu.make_async_copy(staged.at[half], out.at[:, columns, :], sems.at[half])

    @pl.when(step == 0)
    def _():
        weights[...] = omega1[...].astype(jnp.float32).T.astype(jnp.bfloat16)
        to_place = lax.broadcasted_iota(jnp.int32, (size, size), 0)
        from_place = lax.broadcasted_iota(jnp.int32, (size, size), 1)
        wanted = lax.rem(to_place, depth) * share + lax.div(to_place, depth)
        swap[...] = (from_place == wanted).astype(jnp.float32).astype(jnp.bfloat16)

    for slab in range(n_slab):
        natural = received[slab]
        if share % 16:
            natural = natural.astype(jnp.float32)
        natural = natural.reshape(size, LANES).astype(jnp.bfloat16)
        moved = jnp.dot(swap[...], natural, preferred_element_type=jnp.float32).astype(jnp.bfloat16)
        for column in range(share):
            by_row[slab * depth:(slab + 1) * depth, column * LANES:(column + 1) * LANES] = moved[
                column * depth:(column + 1) * depth
            ]
    flat = staged.reshape(share * rank, LANES)
    for half in range(share // part):
        @pl.when(step > 0)
        def _():
            store(step - 1, half).wait()

        for column in range(0, part, 2):
            place = (half * part + column) * LANES
            product = jnp.dot(
                weights[...], by_row[:, place:place + 2 * LANES], preferred_element_type=jnp.float32
            )
            for side in range(2):
                spots = pl.ds(half * rank * part + column + side, rank, stride=part)
                flat[spots, :] = product[:, side * LANES:(side + 1) * LANES]
        store(step, half).start()

    @pl.when(step == steps - 1)
    def _():
        for half in range(share // part):
            store(step, half).wait()


def core(received, omega1):
    n_slab, depth, share, _ = received.shape
    rows, rank = omega1.shape
    tile, part = min(16, share), min(8, share)
    return pl.pallas_call(
        core_kernel,
        grid=(share // tile,),
        out_shape=jax.ShapeDtypeStruct((rank, share, LANES), jnp.float32),
        in_specs=[
            pl.BlockSpec((n_slab, depth, tile, LANES), lambda t: (0, 0, t, 0)),
            pl.BlockSpec((rows, rank), lambda t: (0, 0)),
        ],
        out_specs=pl.BlockSpec(memory_space=pl.ANY),
        scratch_shapes=[
            pltpu.VMEM((rows, tile * LANES), jnp.bfloat16),
            pltpu.VMEM((rank, rows), jnp.bfloat16),
            pltpu.VMEM((depth * tile, depth * tile), jnp.bfloat16),
            pltpu.VMEM((tile // part, rank, part, LANES), jnp.float32),
            pltpu.SemaphoreType.DMA((tile // part,)),
        ],
        compiler_params=pltpu.CompilerParams(vmem_limit_bytes=62 * 2**20),
        cost_estimate=pl.CostEstimate(
            flops=2 * rank * rows * share * LANES,
            bytes_accessed=rank * share * LANES * 4, transcendentals=0,
        ),
        name="core",
    )(received, omega1)


def local(n_slab, blocks, coords, counts, omega1, omega2, omega3):
    own_blocks = blocks[0]
    n_slots, depth, edge, _ = own_blocks.shape
    row = lax.broadcasted_iota(jnp.int32, (8, LANES), 0)
    lane = lax.broadcasted_iota(jnp.int32, (8, LANES), 1)
    corners = jnp.pad(coords[0, 0].T, ((0, 6), (0, LANES - n_slots)))
    meta = jnp.where(row == 2, (lane < counts[0, 0]).astype(jnp.int32), corners)
    omega2 = omega2.reshape(-1, edge, omega2.shape[1])
    omega3 = omega3.reshape(-1, edge, omega3.shape[1])
    received = exchange(own_blocks, meta, omega2, omega3, n_slab, 1)
    return core(received, omega1)


def solution(mesh):
    in_specs = (
        P("grp", None, "slab", None, None),
        P("grp", "slab", None, None),
        P("grp", "slab"),
        P(),
        P(),
        P(),
    )
    out_specs = P(None, "slab", "grp")
    body = functools.partial(local, mesh.shape["slab"])
    return jax.shard_map(body, mesh=mesh, in_specs=in_specs, out_specs=out_specs, check_vma=False)
```
